32 devices in a mesh: groups: 2 (over x), bricks: 16 (over z, y, core).
Axes of the slice: x: 2, y: 2, z: 4, core: 2. Of those that a mesh axis runs over, the one named last changes fastest.
Arguments:
- snapshots: bfloat16 [512, 32, 32, 256], P(('groups', 'bricks')), parts along dimension 0, may hold values from -30 to 30
- material: int32 [512, 1024], P(('groups', 'bricks')), parts along dimension 0, may hold values from 0 to 15
- occupancy: int32 [32, 4], P(('groups', 'bricks')), parts along dimension 0, may hold values 0 or 1
- moduli: bfloat16 [16], replicated, may hold values from 0.19921875 to 5
Outputs:
- energy_gram: float32 [512, 256], P(('groups', 'bricks')), parts along dimension 0
The draws below stay inside these ranges and needn't reach their ends.
There are 2 independent parts, one for each index of `groups`. The reference program is written for one: setup_inputs(seed, part) draws one part's arguments, and reference() takes and returns one part's arrays. A program takes and returns all parts, laid end to end along the dimension named above; an argument that names none is the same for every part. Nothing has to cross between parts.
All inputs are finite; a program needn't handle non-finite values. No bound on the sum of `occupancy` on one device may be relied on, other than what follows from the above.
Results may differ from the reference program's by a relative error of at most 0.0003.
Values may be sent and summed in bfloat16 or wider, within the bound.
A program may use at most 128 MiB of HBM per device.

```python
import math
import jax
import jax.numpy as jnp
from jax import lax

S = 256
ZC = 16
GY = 32
GX = 32
CLASSES = 16
TILES = 4
Z = 256
VOXELS = 262144
N_BRICKS = 16


def draw_rates(sub_key, rate_shape, low_rate, high_rate):
    key_mag, key_sign = jax.random.split(sub_key)
    magnitude = jax.random.uniform(key_mag, rate_shape, jnp.float32, low_rate, high_rate)
    sign_values = jnp.where(jax.random.bernoulli(key_sign, 0.5, rate_shape), 1.0, -1.0)
    return magnitude * sign_values


def draw_snapshots(key, part):
    subkeys = jax.random.split(jax.random.fold_in(key, 7), 10)
    along_z = jnp.arange(Z, dtype=jnp.float32)[:, None, None, None]
    along_y = jnp.arange(GY, dtype=jnp.float32)[None, :, None, None]
    along_x = jnp.arange(GX, dtype=jnp.float32)[None, None, :, None]
    mode_z = draw_rates(subkeys[0], (3, S), 0.03, 0.3)
    mode_y = draw_rates(subkeys[1], (3, S), 0.05, 0.4)
    mode_x = draw_rates(subkeys[2], (3, S), 0.05, 0.4)
    phases = jax.random.uniform(subkeys[3], (3, S), jnp.float32, -math.pi, math.pi)
    shared_rates = draw_rates(subkeys[4], (3,), 0.03, 0.3)
    shared_phase = jax.random.uniform(subkeys[5], (), jnp.float32, -math.pi, math.pi)
    mode_scale = 0.8
    shared_scale = 0.8
    amplitudes = mode_scale * jax.random.truncated_normal(subkeys[6], -2.5, 2.5, (3, S), jnp.float32)
    shared_amp = shared_scale * jax.random.truncated_normal(subkeys[7], -2.5, 2.5, (S,), jnp.float32)
    smooth = shared_amp * jnp.sin(shared_rates[0] * along_z + shared_rates[1] * along_y + shared_rates[2] * along_x + shared_phase)
    for mode_index in range(3):
        argument = mode_z[mode_index] * along_z + mode_y[mode_index] * along_y + mode_x[mode_index] * along_x + phases[mode_index]
        smooth = smooth + amplitudes[mode_index] * jnp.sin(argument)
    full_shape = (Z, GY, GX, S)
    white_noise = 0.2 * jax.random.truncated_normal(subkeys[8], -4.0, 4.0, full_shape, jnp.float32)
    blocks = Z // ZC
    pairing = jax.random.permutation(subkeys[9], blocks)
    block_of_z = jnp.arange(Z, dtype=jnp.int32) // ZC
    block_of_s = jnp.arange(S, dtype=jnp.int32) // (S // blocks)
    spiked = pairing[block_of_z][:, None] == block_of_s[None, :]
    factor = jnp.where(spiked, 3.0, 1.0)[:, None, None, :]
    return jnp.clip(factor * (smooth + white_noise), -30.0, 30.0).astype(jnp.bfloat16)


def plant(drawn, key, least, top_value):
    index_at = [jax.random.randint(jax.random.fold_in(key, axis), (), 0, length) for axis, length in enumerate(drawn.shape)]
    longest = drawn.shape.index(max(drawn.shape))
    next_to = index_at[:longest] + [(index_at[longest] + 1) % drawn.shape[longest]] + index_at[longest + 1:]
    return drawn.at[tuple(index_at)].set(least).at[tuple(next_to)].set(top_value)


def setup_inputs(seed: int = 0, part: int = 0) -> dict:
    splits = jax.random.split(jax.random.key(seed), 5)
    part_keys = jax.random.split(jax.random.fold_in(splits[4], part), 5)
    snapshots = draw_snapshots(jax.random.fold_in(jax.random.fold_in(splits[4], part), 71), part)
    material = plant(jax.random.randint(part_keys[1], (Z, GY * GX), 0, CLASSES), jax.random.fold_in(part_keys[1], 1), 0, CLASSES - 1).astype(jnp.int32)
    occupancy = plant((jax.random.randint(part_keys[2], (N_BRICKS, TILES), 0, 4) < 3).astype(jnp.int32), jax.random.fold_in(part_keys[2], 1), 0, 1)
    moduli = jnp.clip(jnp.exp(jax.random.uniform(splits[3], (CLASSES,), jnp.float32, math.log(0.19921875), math.log(5.0))), 0.19921875, 5.0).astype(jnp.bfloat16)
    return dict(snapshots=snapshots, material=material, occupancy=occupancy, moduli=moduli)


def stencil(padded_field, padded_modulus):
    depth = padded_field.shape[0] - 2
    rows_y = padded_field.shape[1]
    rows_x = padded_field.shape[2]
    field_full = jnp.pad(padded_field, ((0, 0), (1, 1), (1, 1), (0, 0)))
    modulus_full = jnp.pad(padded_modulus, ((0, 0), (1, 1), (1, 1)))
    center = field_full[1:1 + depth, 1:1 + rows_y, 1:1 + rows_x]
    center_mod = modulus_full[1:1 + depth, 1:1 + rows_y, 1:1 + rows_x]
    mod_sum = jnp.zeros_like(center_mod)
    field_sum = jnp.zeros_like(center)
    product_sum = jnp.zeros_like(center)
    total_weight = 0.0
    for shift_z in (-1, 0, 1):
        for shift_y in (-1, 0, 1):
            for shift_x in (-1, 0, 1):
                nonzero = abs(shift_z) + abs(shift_y) + abs(shift_x)
                if nonzero == 0:
                    continue
                weight = (1.0, 0.5, 0.25)[nonzero - 1]
                total_weight = total_weight + weight
                near = field_full[1 + shift_z:1 + shift_z + depth, 1 + shift_y:1 + shift_y + rows_y, 1 + shift_x:1 + shift_x + rows_x]
                near_mod = modulus_full[1 + shift_z:1 + shift_z + depth, 1 + shift_y:1 + shift_y + rows_y, 1 + shift_x:1 + shift_x + rows_x]
                mod_sum = mod_sum + weight * near_mod
                field_sum = field_sum + weight * near
                product_sum = product_sum + weight * near_mod[..., None] * near
    diagonal = 0.5 * (total_weight * center_mod + mod_sum)
    return diagonal[..., None] * center - 0.5 * center_mod[..., None] * field_sum - 0.5 * product_sum


def reference(snapshots, material, occupancy, moduli):
    tiles = occupancy.reshape(N_BRICKS, GY // 16, GX // 16)
    occupied = jnp.repeat(jnp.repeat(jnp.repeat(tiles, ZC, 0), 16, 1), 16, 2)
    occ_bf = occupied.astype(jnp.bfloat16)
    modulus = moduli[material].reshape(Z, GY, GX) * occ_bf
    field = snapshots * occ_bf[..., None]
    field_pad = jnp.pad(field, ((1, 1), (0, 0), (0, 0), (0, 0)))
    modulus_pad = jnp.pad(modulus, ((1, 1), (0, 0), (0, 0)))

    def one_block(total, block):
        start = (block * ZC).astype(jnp.int32)
        piece = lax.dynamic_slice_in_dim(field_pad, start, ZC + 2, 0).astype(jnp.float32)
        piece_mod = lax.dynamic_slice_in_dim(modulus_pad, start, ZC + 2, 0).astype(jnp.float32)
        image = stencil(piece, piece_mod).astype(jnp.bfloat16).reshape(-1, S)
        own = lax.dynamic_slice_in_dim(field, start, ZC, 0).reshape(-1, S)
        term = lax.dot_general(own.astype(jnp.float32), image.astype(jnp.float32), (((0,), (0,)), ((), ())))
        return total + term, None

    total, _ = lax.scan(one_block, jnp.zeros((S, S), jnp.float32), jnp.arange(N_BRICKS, dtype=jnp.int32))
    return total * (1.0 / VOXELS)
```

```python
import functools

import jax
import jax.numpy as jnp
from jax import lax
from jax.experimental import pallas as pl
from jax.experimental.pallas import tpu as pltpu
from jax.sharding import PartitionSpec as P


TRANSPOSED = (((0,), (0,)), ((), ()))


def windows(rows_y):
    found, first = [], 0
    start = 0
    while True:
        start = min(start, rows_y - 8)
        last = rows_y if start + 8 == rows_y else start + 7
        found.append((start, first, last))
        first = last
        if last == rows_y:
            return found
        start = last - 1


def fill_weights(ref, occupied, rows_y, rows_x):
    for start, first, last in windows(rows_y):
        shape = ((last - first) * rows_x, 8 * rows_x)
        row = lax.broadcasted_iota(jnp.int32, shape, 0)
        col = lax.broadcasted_iota(jnp.int32, shape, 1)
        gap_y = jnp.abs(row // rows_x + first - col // rows_x - start)
        gap_x = jnp.abs(row % rows_x - col % rows_x)
        weight = jnp.maximum(2 - gap_y, 0) * jnp.maximum(2 - gap_x, 0)
        here = occupied[:, start * rows_x : (start + 8) * rows_x]
        ref[first * rows_x : last * rows_x, :] = (weight.astype(jnp.float32) * here).astype(
            jnp.bfloat16
        )


def kernel(
    n, rows_y, rows_x, scale,
    snap, material, occupancy, moduli, out,
    field, ring, split, weights, weights_next, columns, total, share, arrived, edge_out, edge_in,
    load_sem, plane_send, plane_recv, edge_send, edge_recv, share_send, share_recv,
):
    me = lax.axis_index("bricks")
    depth, plane, width = snap.shape
    own = out.shape[0]

    loads = [
        pltpu.make_async_copy(snap.at[z], field.at[z], load_sem.at[z]) for z in range(depth)
    ]
    for load in loads:
        load.start()
    barrier = pltpu.get_barrier_semaphore()

    def greet(step, carry):
        pl.semaphore_signal(barrier, inc=1, device_id={"bricks": lax.rem(me + step, n)})
        return carry

    lax.fori_loop(1, n, greet, 0)

    place = lax.broadcasted_iota(jnp.int32, (1, plane), 1)
    at_x, at_y = place % rows_x, place // rows_x
    tile = (at_y // 16) * (rows_x // 16) + at_x // 16
    occupied = jnp.zeros((1, plane), jnp.float32)
    for t in range(occupancy.shape[1]):
        occupied = jnp.where(tile == t, occupancy[0, t].astype(jnp.float32), occupied)
    classes = material[...]
    modulus = jnp.zeros((depth, plane), jnp.float32)
    for c in range(moduli.shape[0]):
        modulus = jnp.where(classes == c, moduli[c], modulus)
    modulus = modulus * occupied
    edge_out[0, 0:1, :] = modulus[0:1]
    edge_out[0, 1:2, :] = occupied
    edge_out[0, 2:8, :] = jnp.zeros((6, plane), jnp.float32)
    edge_out[1, 0:1, :] = modulus[depth - 1 : depth]
    edge_out[1, 1:8, :] = jnp.zeros((7, plane), jnp.float32)

    below, above = lax.rem(me + n - 1, n), lax.rem(me + 1, n)

    def edge_copy(side):
        return pltpu.make_async_remote_copy(
            src_ref=edge_out.at[side],
            dst_ref=edge_in.at[side],
            send_sem=edge_send.at[side],
            recv_sem=edge_recv.at[side],
            device_id={"bricks": below if side == 0 else above},
        )

    def plane_copy():
        return pltpu.make_async_remote_copy(
            src_ref=snap.at[0],
            dst_ref=field.at[depth],
            send_sem=plane_send,
            recv_sem=plane_recv,
            device_id={"bricks": below},
        )

    pl.semaphore_wait(barrier, n - 1)

    @pl.when(me > 0)
    def _():
        edge_copy(0).start()
        plane_copy().start()

    @pl.when(me < n - 1)
    def _():
        edge_copy(1).start()

    @pl.when(me == n - 1)
    def _():
        edge_in[0] = jnp.zeros(edge_in.shape[1:], jnp.float32)
        field[depth] = jnp.zeros(field.shape[1:], jnp.bfloat16)

    @pl.when(me == 0)
    def _():
        edge_in[1] = jnp.zeros(edge_in.shape[1:], jnp.float32)

    fill_weights(weights, occupied, rows_y, rows_x)
    total[...] = jnp.zeros_like(total)
    ring[2] = jnp.zeros(ring.shape[1:], jnp.float32)

    @pl.when(me < n - 1)
    def _():
        edge_copy(0).wait_recv()

    @pl.when(me > 0)
    def _():
        edge_copy(1).wait_recv()

    fill_weights(weights_next, edge_in[0, 1:2, :], rows_y, rows_x)

    moduli_all = jnp.concatenate(
        [modulus, edge_in[0, 0:1, :], edge_in[1, 0:1, :], jnp.zeros((6, plane), jnp.float32)], 0
    )
    summed = moduli_all
    for at, count, step in ((at_x, rows_x, 1), (at_y, rows_y, rows_x)):
        lower = jnp.where(at > 0, pltpu.roll(summed, step, 1), 0.0)
        upper = jnp.where(at < count - 1, pltpu.roll(summed, plane - step, 1), 0.0)
        summed = lower + upper + 2.0 * summed
    around = (
        jnp.concatenate([summed[depth + 1 : depth + 2], summed[: depth - 1]], 0)
        + 2.0 * summed[:depth]
        + summed[1 : depth + 1]
    )
    diagonal = (4.0 * modulus + 0.0625 * around) * occupied
    diagonal_high = diagonal.astype(jnp.bfloat16).astype(jnp.float32)
    gap = jnp.zeros((32 - depth, plane), jnp.float32)
    stack = jnp.concatenate(
        [
            0.125 * moduli_all,
            jnp.zeros((8, plane), jnp.float32),
            diagonal_high,
            gap,
            diagonal - diagonal_high,
            gap,
            jnp.zeros((32, plane), jnp.float32),
        ],
        0,
    )
    columns[...] = stack.T.astype(jnp.bfloat16)

    def convolve(z, table, slot):
        for start, first, last in windows(rows_y):
            rows = slice(first * rows_x, last * rows_x)
            ring[slot, rows, :] = jnp.dot(
                table[rows, :],
                field[z, start * rows_x : (start + 8) * rows_x, :],
                preferred_element_type=jnp.float32,
            )

    def picker(z):
        row = lax.broadcasted_iota(jnp.int32, (128, 256), 0)
        col = lax.broadcasted_iota(jnp.int32, (128, 256), 1)
        is_modulus = (col < 128) & (row == z)
        is_diagonal = (col >= 128) & ((row == z + 32) | (row == z + 64))
        return jnp.where(is_modulus | is_diagonal, 1.0, 0.0).astype(jnp.bfloat16)

    def put(rows, part, value):
        high = value.astype(jnp.bfloat16)
        split[rows, part * 128 : (part + 1) * 128] = high
        split[rows, width + part * 128 : width + (part + 1) * 128] = (
            value - high.astype(jnp.float32)
        ).astype(jnp.bfloat16)

    def add_gram(z):
        total[...] += lax.dot_general(
            field[z], split[...], TRANSPOSED, preferred_element_type=jnp.float32
        )

    def one_plane(z, table):
        older, now, newer = lax.rem(z + 2, 3), lax.rem(z, 3), lax.rem(z + 1, 3)
        pick = picker(z)
        for start, first, last in windows(rows_y):
            rows = slice(first * rows_x, last * rows_x)
            fresh = jnp.dot(
                table[rows, :],
                field[z + 1, start * rows_x : (start + 8) * rows_x, :],
                preferred_element_type=jnp.float32,
            )
            ring[newer, rows, :] = fresh
            spread = jnp.dot(columns[rows, :], pick, preferred_element_type=jnp.float32)
            for part in range(width // 128):
                lanes = slice(part * 128, (part + 1) * 128)
                around = ring[older, rows, lanes] + 2.0 * ring[now, rows, lanes] + fresh[:, lanes]
                value = (
                    spread[:, 128:] * field[z, rows, lanes].astype(jnp.float32)
                    - spread[:, :128] * around
                )
                put(rows, part, value)
        add_gram(z)

    loads[0].wait()
    convolve(0, weights, 0)

    def step(z, carry):
        pltpu.make_async_copy(snap.at[z + 1], field.at[z + 1], load_sem.at[z + 1]).wait()
        one_plane(z, weights)
        return carry

    lax.fori_loop(0, depth - 1, step, 0)

    @pl.when(me < n - 1)
    def _():
        plane_copy().wait_recv()

    one_plane(depth - 1, weights_next)
    pick = picker(depth)
    for start, first, last in windows(rows_y):
        rows = slice(first * rows_x, last * rows_x)
        spread = jnp.dot(columns[rows, :], pick, preferred_element_type=jnp.float32)
        for part in range(width // 128):
            lanes = slice(part * 128, (part + 1) * 128)
            put(rows, part, -spread[:, :128] * ring[(depth - 1) % 3, rows, lanes])
    add_gram(depth)

    half = total[:, :width] + total[:, width:]
    gram = (half + half.T) * scale
    for j in range(n):
        share[j] = gram[j * own : (j + 1) * own, :]

    def share_copy(step):
        peer = lax.rem(me + step, n)
        return pltpu.make_async_remote_copy(
            src_ref=share.at[peer],
            dst_ref=arrived.at[step],
            send_sem=share_send.at[step],
            recv_sem=share_recv.at[step],
            device_id={"bricks": peer},
        )

    def send(step, carry):
        share_copy(step).start()
        return carry

    lax.fori_loop(1, n, send, 0)

    def receive(step, result):
        share_copy(step).wait_recv()
        return result + arrived[step]

    out[...] = lax.fori_loop(1, n, receive, share[me])

    def finish(step, carry):
        share_copy(step).wait_send()
        return carry

    lax.fori_loop(1, n, finish, 0)

    @pl.when(me > 0)
    def _():
        edge_copy(0).wait_send()
        plane_copy().wait_send()

    @pl.when(me < n - 1)
    def _():
        edge_copy(1).wait_send()


def local(snapshots, material, occupancy, moduli):
    depth, rows_y, rows_x, width = snapshots.shape
    plane = rows_y * rows_x
    n = lax.axis_size("bricks")
    own = width // n
    f32, bf16 = jnp.float32, jnp.bfloat16
    vmem = pl.BlockSpec(memory_space=pltpu.VMEM)
    smem = pl.BlockSpec(memory_space=pltpu.SMEM)
    flops = 2 * depth * plane * 256 * (2 * width + 3 * 256)
    return pl.pallas_call(
        functools.partial(kernel, n, rows_y, rows_x, 1.0 / (depth * plane * n)),
        out_shape=jax.ShapeDtypeStruct((own, width), f32),
        in_specs=[pl.BlockSpec(memory_space=pl.ANY), vmem, smem, smem],
        out_specs=vmem,
        scratch_shapes=[
            pltpu.VMEM((depth + 1, plane, width), bf16),
            pltpu.VMEM((3, plane, width), f32),
            pltpu.VMEM((plane, 2 * width), bf16),
            pltpu.VMEM((plane, 8 * rows_x), bf16),
            pltpu.VMEM((plane, 8 * rows_x), bf16),
            pltpu.VMEM((plane, 128), bf16),
            pltpu.VMEM((width, 2 * width), f32),
            pltpu.VMEM((n, own, width), f32),
            pltpu.VMEM((n, own, width), f32),
            pltpu.VMEM((2, 8, plane), f32),
            pltpu.VMEM((2, 8, plane), f32),
            pltpu.SemaphoreType.DMA((depth,)),
            pltpu.SemaphoreType.DMA,
            pltpu.SemaphoreType.DMA,
            pltpu.SemaphoreType.DMA((2,)),
            pltpu.SemaphoreType.DMA((2,)),
            pltpu.SemaphoreType.DMA((n,)),
            pltpu.SemaphoreType.DMA((n,)),
        ],
        compiler_params=pltpu.CompilerParams(
            collective_id=0, has_side_effects=True, vmem_limit_bytes=48 * 1024 * 1024
        ),
        cost_estimate=pl.CostEstimate(
            flops=flops, bytes_accessed=depth * plane * width * 2, transcendentals=0
        ),
    )(
        snapshots.reshape(depth, plane, width),
        material,
        occupancy,
        moduli.astype(f32),
    )


def solution(mesh):
    in_specs = (
        P(("groups", "bricks"), None, None, None),
        P(("groups", "bricks"), None),
        P(("groups", "bricks"), None),
        P(),
    )
    out_specs = P(("groups", "bricks"), None)
    return jax.shard_map(local, mesh=mesh, in_specs=in_specs, out_specs=out_specs, check_vma=False)
```

```python
import functools

import jax
import jax.numpy as jnp
from jax import lax
from jax.experimental import pallas as pl
from jax.experimental.pallas import tpu as pltpu
from jax.sharding import PartitionSpec as P


TRANSPOSED = (((0,), (0,)), ((), ()))


def windows(rows_y):
    found, first = [], 0
    start = 0
    while True:
        start = min(start, rows_y - 8)
        last = rows_y if start + 8 == rows_y else start + 7
        found.append((start, first, last))
        first = last
        if last == rows_y:
            return found
        start = last - 1


def fill_weights(ref, occupied, rows_y, rows_x):
    for start, first, last in windows(rows_y):
        shape = ((last - first) * rows_x, 8 * rows_x)
        row = lax.broadcasted_iota(jnp.int32, shape, 0)
        col = lax.broadcasted_iota(jnp.int32, shape, 1)
        gap_y = jnp.abs(row // rows_x + first - col // rows_x - start)
        gap_x = jnp.abs(row % rows_x - col % rows_x)
        weight = jnp.maximum(2 - gap_y, 0) * jnp.maximum(2 - gap_x, 0)
        here = occupied[:, start * rows_x : (start + 8) * rows_x]
        ref[first * rows_x : last * rows_x, :] = (weight.astype(jnp.float32) * here).astype(
            jnp.bfloat16
        )


def kernel(
    n, rows_y, rows_x, scale,
    snap, material_in, occupancy_in, moduli_in, out,
    field, newest, pair, split, weights, weights_next, columns, total, share, mate, mine, arrived,
    edge_out, edge_in, material, occupancy, moduli,
    load_sem, small_sem, plane_send, plane_recv, edge_send, edge_recv, share_send, share_recv,
    mate_send, mate_recv,
):
    me = lax.axis_index("bricks")
    depth, plane, width = snap.shape
    own = out.shape[0]

    loads = [
        pltpu.make_async_copy(snap.at[z], field.at[z], load_sem.at[z]) for z in range(depth)
    ]
    small = [
        pltpu.make_async_copy(source, target, small_sem.at[i])
        for i, (source, target) in enumerate(
            ((material_in, material), (occupancy_in, occupancy), (moduli_in, moduli))
        )
    ]
    for load in small + loads:
        load.start()
    barrier = pltpu.get_barrier_semaphore()
    below, above = lax.rem(me + n - 1, n), lax.rem(me + 1, n)
    core = lax.rem(me, 2)
    other_core = me + 1 - 2 * core
    for neighbour in (below, above):
        pl.semaphore_signal(barrier, inc=1, device_id={"bricks": neighbour})

    def greet(step, carry):
        pl.semaphore_signal(barrier, inc=1, device_id={"bricks": lax.rem(me + 2 * step, n)})
        return carry

    lax.fori_loop(1, n // 2, greet, 0)
    for load in small:
        load.wait()

    place = lax.broadcasted_iota(jnp.int32, (1, plane), 1)
    at_x, at_y = place % rows_x, place // rows_x
    tile = (at_y // 16) * (rows_x // 16) + at_x // 16
    occupied = jnp.zeros((1, plane), jnp.float32)
    for t in range(occupancy.shape[1]):
        occupied = jnp.where(tile == t, occupancy[0:1, t : t + 1].astype(jnp.float32), occupied)
    classes = material[...]
    modulus = jnp.zeros((depth, plane), jnp.float32)
    for c in range(moduli.shape[1]):
        modulus = jnp.where(classes == c, moduli[0:1, c : c + 1], modulus)
    modulus = modulus * occupied
    edge_out[0, 0:1, :] = modulus[0:1]
    edge_out[0, 1:2, :] = occupied
    edge_out[0, 2:8, :] = jnp.zeros((6, plane), jnp.float32)
    edge_out[1, 0:1, :] = modulus[depth - 1 : depth]
    edge_out[1, 1:8, :] = jnp.zeros((7, plane), jnp.float32)

    def edge_copy(side):
        return pltpu.make_async_remote_copy(
            src_ref=edge_out.at[side],
            dst_ref=edge_in.at[side],
            send_sem=edge_send.at[side],
            recv_sem=edge_recv.at[side],
            device_id={"bricks": below if side == 0 else above},
        )

    def plane_copy():
        return pltpu.make_async_remote_copy(
            src_ref=snap.at[0],
            dst_ref=field.at[depth],
            send_sem=plane_send,
            recv_sem=plane_recv,
            device_id={"bricks": below},
        )

    pl.semaphore_wait(barrier, n // 2 + 1)

    @pl.when(me > 0)
    def _():
        edge_copy(0).start()
        plane_copy().start()

    @pl.when(me < n - 1)
    def _():
        edge_copy(1).start()

    @pl.when(me == n - 1)
    def _():
        edge_in[0] = jnp.zeros(edge_in.shape[1:], jnp.float32)
        field[depth] = jnp.zeros(field.shape[1:], jnp.bfloat16)

    @pl.when(me == 0)
    def _():
        edge_in[1] = jnp.zeros(edge_in.shape[1:], jnp.float32)

    fill_weights(weights, occupied, rows_y, rows_x)
    total[...] = jnp.zeros_like(total)
    split[1] = jnp.zeros(split.shape[1:], jnp.bfloat16)
    loads[0].wait()
    for start, first, last in windows(rows_y):
        rows = slice(first * rows_x, last * rows_x)
        fresh = jnp.dot(
            weights[rows, :],
            field[0, start * rows_x : (start + 8) * rows_x, :],
            preferred_element_type=jnp.float32,
        )
        newest[rows, :] = fresh
        pair[rows, :] = fresh

    @pl.when(me < n - 1)
    def _():
        edge_copy(0).wait_recv()

    @pl.when(me > 0)
    def _():
        edge_copy(1).wait_recv()

    fill_weights(weights_next, edge_in[0, 1:2, :], rows_y, rows_x)

    moduli_all = jnp.concatenate(
        [modulus, edge_in[0, 0:1, :], edge_in[1, 0:1, :], jnp.zeros((6, plane), jnp.float32)], 0
    )
    summed = moduli_all
    for at, count, step in ((at_x, rows_x, 1), (at_y, rows_y, rows_x)):
        lower = jnp.where(at > 0, pltpu.roll(summed, step, 1), 0.0)
        upper = jnp.where(at < count - 1, pltpu.roll(summed, plane - step, 1), 0.0)
        summed = lower + upper + 2.0 * summed
    around = (
        jnp.concatenate([summed[depth + 1 : depth + 2], summed[: depth - 1]], 0)
        + 2.0 * summed[:depth]
        + summed[1 : depth + 1]
    )
    diagonal = (4.0 * modulus + 0.0625 * around) * occupied
    diagonal_high = diagonal.astype(jnp.bfloat16).astype(jnp.float32)
    gap = jnp.zeros((32 - depth, plane), jnp.float32)
    stack = jnp.concatenate(
        [
            0.125 * moduli_all,
            jnp.zeros((8, plane), jnp.float32),
            diagonal_high,
            gap,
            diagonal - diagonal_high,
            gap,
            jnp.zeros((32, plane), jnp.float32),
        ],
        0,
    )
    columns[...] = stack.T.astype(jnp.bfloat16)

    def picker(z):
        row = lax.broadcasted_iota(jnp.int32, (128, 256), 0)
        col = lax.broadcasted_iota(jnp.int32, (128, 256), 1)
        is_modulus = (col < 128) & (row == z)
        is_diagonal = (col >= 128) & ((row == z + 32) | (row == z + 64))
        return jnp.where(is_modulus | is_diagonal, 1.0, 0.0).astype(jnp.bfloat16)

    def put(slot, rows, part, value):
        high = value.astype(jnp.bfloat16)
        split[slot, rows, part * 128 : (part + 1) * 128] = high
        split[slot, rows, width + part * 128 : width + (part + 1) * 128] = (
            value - high.astype(jnp.float32)
        ).astype(jnp.bfloat16)

    def add_gram(z, slot):
        total[...] += lax.dot_general(
            field[z], split[slot], TRANSPOSED, preferred_element_type=jnp.float32
        )

    def one_plane(z, slot, table, last_plane=False):
        pick = picker(z)
        for index, (start, first, last) in enumerate(windows(rows_y)):
            rows = slice(first * rows_x, last * rows_x)
            fresh = jnp.dot(
                table[rows, :],
                field[z + 1, start * rows_x : (start + 8) * rows_x, :],
                preferred_element_type=jnp.float32,
            )
            spread = jnp.dot(columns[rows, :], pick, preferred_element_type=jnp.float32)
            for part in range(width // 128):
                lanes = slice(part * 128, (part + 1) * 128)
                later = newest[rows, lanes] + fresh[:, lanes]
                around = pair[rows, lanes] + later
                if not last_plane:
                    newest[rows, lanes] = fresh[:, lanes]
                    pair[rows, lanes] = later
                value = (
                    spread[:, 128:] * field[z, rows, lanes].astype(jnp.float32)
                    - spread[:, :128] * around
                )
                put(slot, rows, part, value)
            if index == 2:
                add_gram(jnp.maximum(z - 1, 0), 1 - slot)

    def wait_plane(z):
        pltpu.make_async_copy(snap.at[z], field.at[z], load_sem.at[z]).wait()

    def step(i, carry):
        wait_plane(2 * i + 1)
        wait_plane(2 * i + 2)
        one_plane(2 * i, 0, weights)
        one_plane(2 * i + 1, 1, weights)
        return carry

    lax.fori_loop(0, depth // 2 - 1, step, 0)
    wait_plane(depth - 1)
    one_plane(depth - 2, 0, weights)

    @pl.when(me < n - 1)
    def _():
        plane_copy().wait_recv()

    one_plane(depth - 1, 1, weights_next, last_plane=True)
    pick = picker(depth)
    for start, first, last in windows(rows_y):
        rows = slice(first * rows_x, last * rows_x)
        spread = jnp.dot(columns[rows, :], pick, preferred_element_type=jnp.float32)
        for part in range(width // 128):
            lanes = slice(part * 128, (part + 1) * 128)
            put(0, rows, part, -spread[:, :128] * newest[rows, lanes])
    add_gram(depth - 1, 1)
    add_gram(depth, 0)

    half = total[:, :width] + total[:, width:]
    gram = (half + half.T) * scale
    for j in range(n):
        share[j % 2, j // 2] = gram[j * own : (j + 1) * own, :]

    mate_copy = pltpu.make_async_remote_copy(
        src_ref=share.at[1 - core],
        dst_ref=mate,
        send_sem=mate_send,
        recv_sem=mate_recv,
        device_id={"bricks": other_core},
    )
    mate_copy.start()
    mate_copy.wait_recv()
    mine[...] = share[core] + mate[...]

    def share_copy(step):
        peer = lax.rem(me + 2 * step, n)
        return pltpu.make_async_remote_copy(
            src_ref=mine.at[peer // 2],
            dst_ref=arrived.at[step],
            send_sem=share_send.at[step],
            recv_sem=share_recv.at[step],
            device_id={"bricks": peer},
        )

    def send(step, carry):
        share_copy(step).start()
        return carry

    lax.fori_loop(1, n // 2, send, 0)

    def receive(step, result):
        share_copy(step).wait_recv()
        return result + arrived[step]

    out[...] = lax.fori_loop(1, n // 2, receive, mine[me // 2])

    def finish(step, carry):
        share_copy(step).wait_send()
        return carry

    lax.fori_loop(1, n // 2, finish, 0)
    mate_copy.wait_send()

    @pl.when(me > 0)
    def _():
        edge_copy(0).wait_send()
        plane_copy().wait_send()

    @pl.when(me < n - 1)
    def _():
        edge_copy(1).wait_send()


def local(snapshots, material, occupancy, moduli):
    depth, rows_y, rows_x, width = snapshots.shape
    plane = rows_y * rows_x
    n = lax.axis_size("bricks")
    own = width // n
    f32, bf16 = jnp.float32, jnp.bfloat16
    vmem = pl.BlockSpec(memory_space=pltpu.VMEM)
    flops = 2 * depth * plane * 256 * (2 * width + 3 * 256)
    return pl.pallas_call(
        functools.partial(kernel, n, rows_y, rows_x, 1.0 / (depth * plane * n)),
        out_shape=jax.ShapeDtypeStruct((own, width), f32),
        in_specs=[pl.BlockSpec(memory_space=pl.ANY)] * 4,
        out_specs=vmem,
        scratch_shapes=[
            pltpu.VMEM((depth + 1, plane, width), bf16),
            pltpu.VMEM((plane, width), f32),
            pltpu.VMEM((plane, width), f32),
            pltpu.VMEM((2, plane, 2 * width), bf16),
            pltpu.VMEM((plane, 8 * rows_x), bf16),
            pltpu.VMEM((plane, 8 * rows_x), bf16),
            pltpu.VMEM((plane, 128), bf16),
            pltpu.VMEM((width, 2 * width), f32),
            pltpu.VMEM((2, n // 2, own, width), f32),
            pltpu.VMEM((n // 2, own, width), f32),
            pltpu.VMEM((n // 2, own, width), f32),
            pltpu.VMEM((n // 2, own, width), f32),
            pltpu.VMEM((2, 8, plane), f32),
            pltpu.VMEM((2, 8, plane), f32),
            pltpu.VMEM(material.shape, jnp.int32),
            pltpu.VMEM(occupancy.shape, jnp.int32),
            pltpu.VMEM((1, moduli.shape[0]), f32),
            pltpu.SemaphoreType.DMA((depth,)),
            pltpu.SemaphoreType.DMA((3,)),
            pltpu.SemaphoreType.DMA,
            pltpu.SemaphoreType.DMA,
            pltpu.SemaphoreType.DMA((2,)),
            pltpu.SemaphoreType.DMA((2,)),
            pltpu.SemaphoreType.DMA((n // 2,)),
            pltpu.SemaphoreType.DMA((n // 2,)),
            pltpu.SemaphoreType.DMA,
            pltpu.SemaphoreType.DMA,
        ],
        compiler_params=pltpu.CompilerParams(
            collective_id=0, has_side_effects=True, vmem_limit_bytes=64 * 1024 * 1024
        ),
        cost_estimate=pl.CostEstimate(
            flops=flops, bytes_accessed=depth * plane * width * 2, transcendentals=0
        ),
    )(
        snapshots.reshape(depth, plane, width),
        material,
        occupancy,
        moduli.astype(f32).reshape(1, -1),
    )


def solution(mesh):
    in_specs = (
        P(("groups", "bricks"), None, None, None),
        P(("groups", "bricks"), None),
        P(("groups", "bricks"), None),
        P(),
    )
    out_specs = P(("groups", "bricks"), None)
    return jax.shard_map(local, mesh=mesh, in_specs=in_specs, out_specs=out_specs, check_vma=False)
```

```python
import functools

import jax
import jax.numpy as jnp
from jax import lax
from jax.experimental import pallas as pl
from jax.experimental.pallas import tpu as pltpu
from jax.sharding import PartitionSpec as P


TRANSPOSED = (((0,), (0,)), ((), ()))


def windows(rows_y):
    found, first = [], 0
    start = 0
    while True:
        start = min(start, rows_y - 8)
        last = rows_y if start + 8 == rows_y else start + 7
        found.append((start, first, last))
        first = last
        if last == rows_y:
            return found
        start = last - 1


def fill_weights(ref, occupied, rows_y, rows_x):
    for start, first, last in windows(rows_y):
        shape = ((last - first) * rows_x, 8 * rows_x)
        row = lax.broadcasted_iota(jnp.int32, shape, 0)
        col = lax.broadcasted_iota(jnp.int32, shape, 1)
        gap_y = jnp.abs(row // rows_x + first - col // rows_x - start)
        gap_x = jnp.abs(row % rows_x - col % rows_x)
        weight = jnp.maximum(2 - gap_y, 0) * jnp.maximum(2 - gap_x, 0)
        here = occupied[:, start * rows_x : (start + 8) * rows_x]
        ref[first * rows_x : last * rows_x, :] = (weight.astype(jnp.float32) * here).astype(
            jnp.bfloat16
        )


def kernel(
    n, rows_y, rows_x, scale,
    snap, material_in, occupancy_in, moduli_in, out,
    field, older, newest, around_first, split, weights, weights_next, columns, total, share, mate, mine, arrived,
    edge_out, edge_in, material, occupancy, moduli,
    load_sem, small_sem, plane_send, plane_recv, edge_send, edge_recv, share_send, share_recv,
    mate_send, mate_recv,
):
    me = lax.axis_index("bricks")
    depth, plane, width = snap.shape
    own = out.shape[0]

    loads = [
        pltpu.make_async_copy(snap.at[z], field.at[z], load_sem.at[z]) for z in range(depth)
    ]
    small = [
        pltpu.make_async_copy(source, target, small_sem.at[i])
        for i, (source, target) in enumerate(
            ((material_in, material), (occupancy_in, occupancy), (moduli_in, moduli))
        )
    ]
    for load in small + loads:
        load.start()
    barrier = pltpu.get_barrier_semaphore()
    below, above = lax.rem(me + n - 1, n), lax.rem(me + 1, n)
    core = lax.rem(me, 2)
    other_core = me + 1 - 2 * core
    for neighbour in (below, above):
        pl.semaphore_signal(barrier, inc=1, device_id={"bricks": neighbour})

    def greet(step, carry):
        pl.semaphore_signal(barrier, inc=1, device_id={"bricks": lax.rem(me + 2 * step, n)})
        return carry

    lax.fori_loop(1, n // 2, greet, 0)
    for load in small:
        load.wait()

    place = lax.broadcasted_iota(jnp.int32, (1, plane), 1)
    at_x, at_y = place % rows_x, place // rows_x
    tile = (at_y // 16) * (rows_x // 16) + at_x // 16
    occupied = jnp.zeros((1, plane), jnp.float32)
    for t in range(occupancy.shape[1]):
        occupied = jnp.where(tile == t, occupancy[0:1, t : t + 1].astype(jnp.float32), occupied)
    classes = material[...]
    modulus = jnp.zeros((depth, plane), jnp.float32)
    for c in range(moduli.shape[1]):
        modulus = jnp.where(classes == c, moduli[0:1, c : c + 1].astype(jnp.float32), modulus)
    modulus = modulus * occupied
    edge_out[0, 0:1, :] = modulus[0:1]
    edge_out[0, 1:2, :] = occupied
    edge_out[0, 2:8, :] = jnp.zeros((6, plane), jnp.float32)
    edge_out[1, 0:1, :] = modulus[depth - 1 : depth]
    edge_out[1, 1:8, :] = jnp.zeros((7, plane), jnp.float32)

    def edge_copy(side):
        return pltpu.make_async_remote_copy(
            src_ref=edge_out.at[side],
            dst_ref=edge_in.at[side],
            send_sem=edge_send.at[side],
            recv_sem=edge_recv.at[side],
            device_id={"bricks": below if side == 0 else above},
        )

    def plane_copy():
        return pltpu.make_async_remote_copy(
            src_ref=snap.at[0],
            dst_ref=field.at[depth],
            send_sem=plane_send,
            recv_sem=plane_recv,
            device_id={"bricks": below},
        )

    fill_weights(weights, occupied, rows_y, rows_x)
    total[...] = jnp.zeros_like(total)

    def chunks():
        for start, first, last in windows(rows_y):
            yield (
                slice(first * rows_x, last * rows_x),
                slice(start * rows_x, (start + 8) * rows_x),
            )

    def convolve(table, z, rows, window):
        return jnp.dot(
            table[rows, :], field[z, window, :], preferred_element_type=jnp.float32
        )

    loads[0].wait()
    loads[1].wait()
    for rows, window in chunks():
        plane_0 = convolve(weights, 0, rows, window)
        plane_1 = convolve(weights, 1, rows, window)
        older[rows, :] = plane_0
        newest[rows, :] = plane_1
        around_first[rows, :] = 2.0 * plane_0 + plane_1

    pl.semaphore_wait(barrier, n // 2 + 1)

    @pl.when(me > 0)
    def _():
        edge_copy(0).start()
        plane_copy().start()

    @pl.when(me < n - 1)
    def _():
        edge_copy(1).start()

    @pl.when(me == n - 1)
    def _():
        edge_in[0] = jnp.zeros(edge_in.shape[1:], jnp.float32)
        field[depth] = jnp.zeros(field.shape[1:], jnp.bfloat16)

    @pl.when(me == 0)
    def _():
        edge_in[1] = jnp.zeros(edge_in.shape[1:], jnp.float32)

    def fill_columns(next_plane, last_plane):
        moduli_all = jnp.concatenate(
            [modulus, next_plane, last_plane, jnp.zeros((6, plane), jnp.float32)], 0
        )
        summed = moduli_all
        for at, count, step in ((at_x, rows_x, 1), (at_y, rows_y, rows_x)):
            lower = jnp.where(at > 0, pltpu.roll(summed, step, 1), 0.0)
            upper = jnp.where(at < count - 1, pltpu.roll(summed, plane - step, 1), 0.0)
            summed = lower + upper + 2.0 * summed
        around = (
            jnp.concatenate([summed[depth + 1 : depth + 2], summed[: depth - 1]], 0)
            + 2.0 * summed[:depth]
            + summed[1 : depth + 1]
        )
        diagonal = (4.0 * modulus + 0.0625 * around) * occupied
        diagonal_high = diagonal.astype(jnp.bfloat16).astype(jnp.float32)
        gap = jnp.zeros((32 - depth, plane), jnp.float32)
        stack = jnp.concatenate(
            [
                0.125 * moduli_all,
                jnp.zeros((8, plane), jnp.float32),
                diagonal_high,
                gap,
                diagonal - diagonal_high,
                gap,
                jnp.zeros((32, plane), jnp.float32),
            ],
            0,
        )
        columns[...] = stack.T.astype(jnp.bfloat16)

    nothing = jnp.zeros((1, plane), jnp.float32)
    fill_columns(nothing, nothing)

    def picker(z):
        row = lax.broadcasted_iota(jnp.int32, (128, 256), 0)
        col = lax.broadcasted_iota(jnp.int32, (128, 256), 1)
        is_modulus = (col < 128) & (row == z)
        is_diagonal = (col >= 128) & ((row == z + 32) | (row == z + 64))
        return jnp.where(is_modulus | is_diagonal, 1.0, 0.0).astype(jnp.bfloat16)

    def put(slot, place, rows, part, value):
        rows = slice(place * plane + rows.start, place * plane + rows.stop)
        high = value.astype(jnp.bfloat16)
        split[slot, rows, part * 128 : (part + 1) * 128] = high
        split[slot, rows, width + part * 128 : width + (part + 1) * 128] = (
            value - high.astype(jnp.float32)
        ).astype(jnp.bfloat16)

    def parts():
        for part in range(width // 128):
            yield part, slice(part * 128, (part + 1) * 128)

    def spread_over(pick, rows):
        both = jnp.dot(columns[rows, :], pick, preferred_element_type=jnp.float32)
        return both[:, :128], both[:, 128:]

    def add_gram(z, slot, planes=2):
        total[...] += lax.dot_general(
            field[pl.ds(z, planes)].reshape(planes * plane, width),
            split[slot, : planes * plane, :],
            TRANSPOSED,
            preferred_element_type=jnp.float32,
        )

    def wait_plane(z):
        pltpu.make_async_copy(snap.at[z], field.at[z], load_sem.at[z]).wait()

    def two_planes(z, slot, gram_before=True):
        pick_a, pick_b = picker(z), picker(z + 1)
        for index, (rows, window) in enumerate(chunks()):
            fresh_a = convolve(weights, z + 1, rows, window)
            fresh_b = convolve(weights, z + 2, rows, window)
            m_a, d_a = spread_over(pick_a, rows)
            m_b, d_b = spread_over(pick_b, rows)
            for part, lanes in parts():
                before, now = older[rows, lanes], newest[rows, lanes]
                first, second = fresh_a[:, lanes], fresh_b[:, lanes]
                older[rows, lanes] = first
                newest[rows, lanes] = second
                middle = now + first
                around_a = (before + now) + middle
                around_b = middle + (first + second)
                here_a = field[z, rows, lanes].astype(jnp.float32)
                here_b = field[z + 1, rows, lanes].astype(jnp.float32)
                put(slot, 0, rows, part, d_a * here_a - m_a * around_a)
                put(slot, 1, rows, part, d_b * here_b - m_b * around_b)
            if index == 2 and gram_before:
                add_gram(z - 2, 1 - slot)

    wait_plane(2)
    wait_plane(3)
    two_planes(1, 0, gram_before=False)

    def step(i, carry):
        for ahead in range(6, 10):
            wait_plane(4 * i + ahead - 2)
        two_planes(4 * i + 3, 1)
        two_planes(4 * i + 5, 0)
        return carry

    lax.fori_loop(0, (depth - 4) // 4, step, 0)

    @pl.when(me < n - 1)
    def _():
        edge_copy(0).wait_recv()
        plane_copy().wait_recv()

    @pl.when(me > 0)
    def _():
        edge_copy(1).wait_recv()

    fill_weights(weights_next, edge_in[0, 1:2, :], rows_y, rows_x)
    fill_columns(edge_in[0, 0:1, :], edge_in[1, 0:1, :])
    pick_a, pick_b = picker(depth - 1), picker(depth)
    for index, (rows, window) in enumerate(chunks()):
        fresh = convolve(weights_next, depth, rows, window)
        m_a, d_a = spread_over(pick_a, rows)
        m_b, _ = spread_over(pick_b, rows)
        for part, lanes in parts():
            now = newest[rows, lanes]
            around = older[rows, lanes] + 2.0 * now + fresh[:, lanes]
            here = field[depth - 1, rows, lanes].astype(jnp.float32)
            put(1, 0, rows, part, d_a * here - m_a * around)
            put(1, 1, rows, part, -m_b * now)
        if index == 2:
            add_gram(depth - 3, 0)
    pick = picker(0)
    for index, (rows, window) in enumerate(chunks()):
        m, d = spread_over(pick, rows)
        for part, lanes in parts():
            here = field[0, rows, lanes].astype(jnp.float32)
            put(0, 0, rows, part, d * here - m * around_first[rows, lanes])
        if index == 2:
            add_gram(depth - 1, 1)
    add_gram(0, 0, planes=1)

    half = total[:, :width] + total[:, width:]
    gram = (half + half.T) * scale
    for j in range(n):
        share[j % 2, j // 2] = gram[j * own : (j + 1) * own, :]

    mate_copy = pltpu.make_async_remote_copy(
        src_ref=share.at[1 - core],
        dst_ref=mate,
        send_sem=mate_send,
        recv_sem=mate_recv,
        device_id={"bricks": other_core},
    )
    mate_copy.start()
    mate_copy.wait_recv()
    mine[...] = share[core] + mate[...]

    def share_copy(step):
        peer = lax.rem(me + 2 * step, n)
        return pltpu.make_async_remote_copy(
            src_ref=mine.at[peer // 2],
            dst_ref=arrived.at[step],
            send_sem=share_send.at[step],
            recv_sem=share_recv.at[step],
            device_id={"bricks": peer},
        )

    def send(step, carry):
        share_copy(step).start()
        return carry

    lax.fori_loop(1, n // 2, send, 0)

    def receive(step, result):
        share_copy(step).wait_recv()
        return result + arrived[step]

    out[...] = lax.fori_loop(1, n // 2, receive, mine[me // 2])

    def finish(step, carry):
        share_copy(step).wait_send()
        return carry

    lax.fori_loop(1, n // 2, finish, 0)
    mate_copy.wait_send()

    @pl.when(me > 0)
    def _():
        edge_copy(0).wait_send()
        plane_copy().wait_send()

    @pl.when(me < n - 1)
    def _():
        edge_copy(1).wait_send()


def local(snapshots, material, occupancy, moduli):
    depth, rows_y, rows_x, width = snapshots.shape
    plane = rows_y * rows_x
    n = lax.axis_size("bricks")
    own = width // n
    f32, bf16 = jnp.float32, jnp.bfloat16
    vmem = pl.BlockSpec(memory_space=pltpu.VMEM)
    flops = 2 * depth * plane * 256 * (2 * width + 3 * 256)
    return pl.pallas_call(
        functools.partial(kernel, n, rows_y, rows_x, 1.0 / (depth * plane * n)),
        out_shape=jax.ShapeDtypeStruct((own, width), f32),
        in_specs=[pl.BlockSpec(memory_space=pl.ANY)] * 4,
        out_specs=vmem,
        scratch_shapes=[
            pltpu.VMEM((depth + 1, plane, width), bf16),
            pltpu.VMEM((plane, width), f32),
            pltpu.VMEM((plane, width), f32),
            pltpu.VMEM((plane, width), f32),
            pltpu.VMEM((2, 2 * plane, 2 * width), bf16),
            pltpu.VMEM((plane, 8 * rows_x), bf16),
            pltpu.VMEM((plane, 8 * rows_x), bf16),
            pltpu.VMEM((plane, 128), bf16),
            pltpu.VMEM((width, 2 * width), f32),
            pltpu.VMEM((2, n // 2, own, width), f32),
            pltpu.VMEM((n // 2, own, width), f32),
            pltpu.VMEM((n // 2, own, width), f32),
            pltpu.VMEM((n // 2, own, width), f32),
            pltpu.VMEM((2, 8, plane), f32),
            pltpu.VMEM((2, 8, plane), f32),
            pltpu.VMEM(material.shape, jnp.int32),
            pltpu.VMEM(occupancy.shape, jnp.int32),
            pltpu.VMEM((1, moduli.shape[0]), bf16),
            pltpu.SemaphoreType.DMA((depth,)),
            pltpu.SemaphoreType.DMA((3,)),
            pltpu.SemaphoreType.DMA,
            pltpu.SemaphoreType.DMA,
            pltpu.SemaphoreType.DMA((2,)),
            pltpu.SemaphoreType.DMA((2,)),
            pltpu.SemaphoreType.DMA((n // 2,)),
            pltpu.SemaphoreType.DMA((n // 2,)),
            pltpu.SemaphoreType.DMA,
            pltpu.SemaphoreType.DMA,
        ],
        compiler_params=pltpu.CompilerParams(
            collective_id=0, has_side_effects=True, vmem_limit_bytes=64 * 1024 * 1024
        ),
        cost_estimate=pl.CostEstimate(
            flops=flops, bytes_accessed=depth * plane * width * 2, transcendentals=0
        ),
    )(
        snapshots.reshape(depth, plane, width),
        material,
        occupancy,
        moduli.reshape(1, -1),
    )


def solution(mesh):
    in_specs = (
        P(("groups", "bricks"), None, None, None),
        P(("groups", "bricks"), None),
        P(("groups", "bricks"), None),
        P(),
    )
    out_specs = P(("groups", "bricks"), None)
    return jax.shard_map(local, mesh=mesh, in_specs=in_specs, out_specs=out_specs, check_vma=False)
```

```python
import functools

import jax
import jax.numpy as jnp
from jax import lax
from jax.experimental import pallas as pl
from jax.experimental.pallas import tpu as pltpu
from jax.sharding import PartitionSpec as P


TRANSPOSED = (((0,), (0,)), ((), ()))


def windows(rows_y):
    found, first = [], 0
    start = 0
    while True:
        start = min(start, rows_y - 8)
        last = rows_y if start + 8 == rows_y else start + 7
        found.append((start, first, last))
        first = last
        if last == rows_y:
            return found
        start = last - 1


def fill_weights(ref, occupied, rows_y, rows_x):
    for start, first, last in windows(rows_y):
        shape = ((last - first) * rows_x, 8 * rows_x)
        row = lax.broadcasted_iota(jnp.int32, shape, 0)
        col = lax.broadcasted_iota(jnp.int32, shape, 1)
        gap_y = jnp.abs(row // rows_x + first - col // rows_x - start)
        gap_x = jnp.abs(row % rows_x - col % rows_x)
        weight = jnp.maximum(2 - gap_y, 0) * jnp.maximum(2 - gap_x, 0)
        here = occupied[:, start * rows_x : (start + 8) * rows_x]
        ref[first * rows_x : last * rows_x, :] = (weight.astype(jnp.float32) * here).astype(
            jnp.bfloat16
        )


def kernel(
    n, rows_y, rows_x, scale,
    snap, material_in, occupancy_in, moduli_in, out,
    field, older, newest, around_first, split, weights, weights_next, columns, total, share, mate, mine, arrived,
    edge_out, edge_in, material, occupancy, moduli,
    load_sem, small_sem, plane_send, plane_recv, edge_send, edge_recv, share_send, share_recv,
    mate_send, mate_recv,
):
    me = lax.axis_index("bricks")
    depth, plane, width = snap.shape
    own = out.shape[0]

    loads = [
        pltpu.make_async_copy(snap.at[z], field.at[z], load_sem.at[z]) for z in range(depth)
    ]
    small = [
        pltpu.make_async_copy(source, target, small_sem.at[i])
        for i, (source, target) in enumerate(
            ((material_in, material), (occupancy_in, occupancy), (moduli_in, moduli))
        )
    ]
    for load in small + loads:
        load.start()
    barrier = pltpu.get_barrier_semaphore()
    below, above = lax.rem(me + n - 1, n), lax.rem(me + 1, n)
    core = lax.rem(me, 2)
    other_core = me + 1 - 2 * core
    for neighbour in (below, above):
        pl.semaphore_signal(barrier, inc=1, device_id={"bricks": neighbour})

    def greet(step, carry):
        pl.semaphore_signal(barrier, inc=1, device_id={"bricks": lax.rem(me + 2 * step, n)})
        return carry

    lax.fori_loop(1, n // 2, greet, 0)
    for load in small:
        load.wait()

    place = lax.broadcasted_iota(jnp.int32, (1, plane), 1)
    at_x, at_y = place % rows_x, place // rows_x
    tile = (at_y // 16) * (rows_x // 16) + at_x // 16
    occupied = jnp.zeros((1, plane), jnp.float32)
    for t in range(occupancy.shape[1]):
        occupied = jnp.where(tile == t, occupancy[0:1, t : t + 1].astype(jnp.float32), occupied)
    classes = material[...]
    modulus = jnp.zeros((depth, plane), jnp.float32)
    for c in range(moduli.shape[1]):
        modulus = jnp.where(classes == c, moduli[0:1, c : c + 1].astype(jnp.float32), modulus)
    modulus = modulus * occupied
    edge_out[0, 0:1, :] = modulus[0:1]
    edge_out[0, 1:2, :] = occupied
    edge_out[0, 2:8, :] = jnp.zeros((6, plane), jnp.float32)
    edge_out[1, 0:1, :] = modulus[depth - 1 : depth]
    edge_out[1, 1:8, :] = jnp.zeros((7, plane), jnp.float32)

    def edge_copy(side):
        return pltpu.make_async_remote_copy(
            src_ref=edge_out.at[side],
            dst_ref=edge_in.at[side],
            send_sem=edge_send.at[side],
            recv_sem=edge_recv.at[side],
            device_id={"bricks": below if side == 0 else above},
        )

    def plane_copy():
        return pltpu.make_async_remote_copy(
            src_ref=snap.at[0],
            dst_ref=field.at[depth],
            send_sem=plane_send,
            recv_sem=plane_recv,
            device_id={"bricks": below},
        )

    fill_weights(weights, occupied, rows_y, rows_x)
    total[...] = jnp.zeros_like(total)

    def chunks():
        for start, first, last in windows(rows_y):
            yield (
                slice(first * rows_x, last * rows_x),
                slice(start * rows_x, (start + 8) * rows_x),
            )

    def convolve(table, z, rows, window):
        return jnp.dot(
            table[rows, :], field[z, window, :], preferred_element_type=jnp.float32
        )

    loads[0].wait()
    loads[1].wait()
    for rows, window in chunks():
        plane_0 = convolve(weights, 0, rows, window)
        plane_1 = convolve(weights, 1, rows, window)
        older[rows, :] = plane_0
        newest[rows, :] = plane_1
        around_first[rows, :] = 2.0 * plane_0 + plane_1

    pl.semaphore_wait(barrier, n // 2 + 1)

    @pl.when(me > 0)
    def _():
        edge_copy(0).start()
        plane_copy().start()

    @pl.when(me < n - 1)
    def _():
        edge_copy(1).start()

    @pl.when(me == n - 1)
    def _():
        edge_in[0] = jnp.zeros(edge_in.shape[1:], jnp.float32)
        field[depth] = jnp.zeros(field.shape[1:], jnp.bfloat16)

    @pl.when(me == 0)
    def _():
        edge_in[1] = jnp.zeros(edge_in.shape[1:], jnp.float32)

    def fill_columns(next_plane, last_plane, copies):
        moduli_all = jnp.concatenate(
            [modulus, next_plane, last_plane, jnp.zeros((6, plane), jnp.float32)], 0
        )
        summed = moduli_all
        for at, count, step in ((at_x, rows_x, 1), (at_y, rows_y, rows_x)):
            lower = jnp.where(at > 0, pltpu.roll(summed, step, 1), 0.0)
            upper = jnp.where(at < count - 1, pltpu.roll(summed, plane - step, 1), 0.0)
            summed = lower + upper + 2.0 * summed
        around = (
            jnp.concatenate([summed[depth + 1 : depth + 2], summed[: depth - 1]], 0)
            + 2.0 * summed[:depth]
            + summed[1 : depth + 1]
        )
        diagonal = (4.0 * modulus + 0.0625 * around) * occupied
        stack = jnp.concatenate(
            [
                0.125 * moduli_all,
                jnp.zeros((8, plane), jnp.float32),
                diagonal,
                jnp.zeros((96 - depth, plane), jnp.float32),
            ],
            0,
        )
        upright = stack.T
        columns[0] = upright
        for copy in range(1, copies):
            columns[copy] = pltpu.roll(upright, 128 - 4 * copy, 1)

    nothing = jnp.zeros((1, plane), jnp.float32)
    fill_columns(nothing, nothing, columns.shape[0])

    def put(slot, place, rows, part, value):
        rows = slice(place * plane + rows.start, place * plane + rows.stop)
        high = value.astype(jnp.bfloat16)
        split[slot, rows, part * 128 : (part + 1) * 128] = high
        split[slot, rows, width + part * 128 : width + (part + 1) * 128] = (
            value - high.astype(jnp.float32)
        ).astype(jnp.bfloat16)

    def parts():
        for part in range(width // 128):
            yield part, slice(part * 128, (part + 1) * 128)

    def spread_over(copy, lane, rows):
        shape = (rows.stop - rows.start, 128)
        m = columns[copy, rows, lane : lane + 1]
        d = columns[copy, rows, lane + 32 : lane + 33]
        return jnp.broadcast_to(m, shape), jnp.broadcast_to(d, shape)

    def add_gram(z, slot, planes=2):
        total[...] += lax.dot_general(
            field[pl.ds(z, planes)].reshape(planes * plane, width),
            split[slot, : planes * plane, :],
            TRANSPOSED,
            preferred_element_type=jnp.float32,
        )

    def wait_plane(z):
        pltpu.make_async_copy(snap.at[z], field.at[z], load_sem.at[z]).wait()

    def two_planes(z, slot, copy, lane, gram_before=True):
        for index, (rows, window) in enumerate(chunks()):
            fresh_a = convolve(weights, z + 1, rows, window)
            fresh_b = convolve(weights, z + 2, rows, window)
            m_a, d_a = spread_over(copy, lane, rows)
            m_b, d_b = spread_over(copy, lane + 1, rows)
            for part, lanes in parts():
                before, now = older[rows, lanes], newest[rows, lanes]
                first, second = fresh_a[:, lanes], fresh_b[:, lanes]
                older[rows, lanes] = first
                newest[rows, lanes] = second
                middle = now + first
                around_a = (before + now) + middle
                around_b = middle + (first + second)
                here_a = field[z, rows, lanes].astype(jnp.float32)
                here_b = field[z + 1, rows, lanes].astype(jnp.float32)
                put(slot, 0, rows, part, d_a * here_a - m_a * around_a)
                put(slot, 1, rows, part, d_b * here_b - m_b * around_b)
            if index == 2 and gram_before:
                add_gram(z - 2, 1 - slot)

    wait_plane(2)
    wait_plane(3)
    two_planes(1, 0, 0, 1, gram_before=False)

    def step(i, carry):
        for ahead in range(6, 10):
            wait_plane(4 * i + ahead - 2)
        two_planes(4 * i + 3, 1, i, 3)
        two_planes(4 * i + 5, 0, i, 5)
        return carry

    lax.fori_loop(0, (depth - 4) // 4, step, 0)

    @pl.when(me < n - 1)
    def _():
        edge_copy(0).wait_recv()
        plane_copy().wait_recv()

    @pl.when(me > 0)
    def _():
        edge_copy(1).wait_recv()

    fill_weights(weights_next, edge_in[0, 1:2, :], rows_y, rows_x)
    fill_columns(edge_in[0, 0:1, :], edge_in[1, 0:1, :], 1)
    for index, (rows, window) in enumerate(chunks()):
        fresh = convolve(weights_next, depth, rows, window)
        m_a, d_a = spread_over(0, depth - 1, rows)
        m_b, _ = spread_over(0, depth, rows)
        for part, lanes in parts():
            now = newest[rows, lanes]
            around = older[rows, lanes] + 2.0 * now + fresh[:, lanes]
            here = field[depth - 1, rows, lanes].astype(jnp.float32)
            put(1, 0, rows, part, d_a * here - m_a * around)
            put(1, 1, rows, part, -m_b * now)
        if index == 2:
            add_gram(depth - 3, 0)
    for index, (rows, window) in enumerate(chunks()):
        m, d = spread_over(0, 0, rows)
        for part, lanes in parts():
            here = field[0, rows, lanes].astype(jnp.float32)
            put(0, 0, rows, part, d * here - m * around_first[rows, lanes])
        if index == 2:
            add_gram(depth - 1, 1)
    add_gram(0, 0, planes=1)

    half = total[:, :width] + total[:, width:]
    gram = (half + half.T) * scale
    for j in range(n):
        share[j % 2, j // 2] = gram[j * own : (j + 1) * own, :]

    mate_copy = pltpu.make_async_remote_copy(
        src_ref=share.at[1 - core],
        dst_ref=mate,
        send_sem=mate_send,
        recv_sem=mate_recv,
        device_id={"bricks": other_core},
    )
    mate_copy.start()
    mate_copy.wait_recv()
    mine[...] = share[core] + mate[...]

    def share_copy(step):
        peer = lax.rem(me + 2 * step, n)
        return pltpu.make_async_remote_copy(
            src_ref=mine.at[peer // 2],
            dst_ref=arrived.at[step],
            send_sem=share_send.at[step],
            recv_sem=share_recv.at[step],
            device_id={"bricks": peer},
        )

    def send(step, carry):
        share_copy(step).start()
        return carry

    lax.fori_loop(1, n // 2, send, 0)

    def receive(step, result):
        share_copy(step).wait_recv()
        return result + arrived[step]

    out[...] = lax.fori_loop(1, n // 2, receive, mine[me // 2])

    def finish(step, carry):
        share_copy(step).wait_send()
        return carry

    lax.fori_loop(1, n // 2, finish, 0)
    mate_copy.wait_send()

    @pl.when(me > 0)
    def _():
        edge_copy(0).wait_send()
        plane_copy().wait_send()

    @pl.when(me < n - 1)
    def _():
        edge_copy(1).wait_send()


def local(snapshots, material, occupancy, moduli):
    depth, rows_y, rows_x, width = snapshots.shape
    plane = rows_y * rows_x
    n = lax.axis_size("bricks")
    own = width // n
    f32, bf16 = jnp.float32, jnp.bfloat16
    vmem = pl.BlockSpec(memory_space=pltpu.VMEM)
    flops = 2 * depth * plane * 256 * (2 * width + 3 * 256)
    return pl.pallas_call(
        functools.partial(kernel, n, rows_y, rows_x, 1.0 / (depth * plane * n)),
        out_shape=jax.ShapeDtypeStruct((own, width), f32),
        in_specs=[pl.BlockSpec(memory_space=pl.ANY)] * 4,
        out_specs=vmem,
        scratch_shapes=[
            pltpu.VMEM((depth + 1, plane, width), bf16),
            pltpu.VMEM((plane, width), f32),
            pltpu.VMEM((plane, width), f32),
            pltpu.VMEM((plane, width), f32),
            pltpu.VMEM((2, 2 * plane, 2 * width), bf16),
            pltpu.VMEM((plane, 8 * rows_x), bf16),
            pltpu.VMEM((plane, 8 * rows_x), bf16),
            pltpu.VMEM(((depth - 4) // 4, plane, 128), f32),
            pltpu.VMEM((width, 2 * width), f32),
            pltpu.VMEM((2, n // 2, own, width), f32),
            pltpu.VMEM((n // 2, own, width), f32),
            pltpu.VMEM((n // 2, own, width), f32),
            pltpu.VMEM((n // 2, own, width), f32),
            pltpu.VMEM((2, 8, plane), f32),
            pltpu.VMEM((2, 8, plane), f32),
            pltpu.VMEM(material.shape, jnp.int32),
            pltpu.VMEM(occupancy.shape, jnp.int32),
            pltpu.VMEM((1, moduli.shape[0]), bf16),
            pltpu.SemaphoreType.DMA((depth,)),
            pltpu.SemaphoreType.DMA((3,)),
            pltpu.SemaphoreType.DMA,
            pltpu.SemaphoreType.DMA,
            pltpu.SemaphoreType.DMA((2,)),
            pltpu.SemaphoreType.DMA((2,)),
            pltpu.SemaphoreType.DMA((n // 2,)),
            pltpu.SemaphoreType.DMA((n // 2,)),
            pltpu.SemaphoreType.DMA,
            pltpu.SemaphoreType.DMA,
        ],
        compiler_params=pltpu.CompilerParams(
            collective_id=0, has_side_effects=True, vmem_limit_bytes=64 * 1024 * 1024
        ),
        cost_estimate=pl.CostEstimate(
            flops=flops, bytes_accessed=depth * plane * width * 2, transcendentals=0
        ),
    )(
        snapshots.reshape(depth, plane, width),
        material,
        occupancy,
        moduli.reshape(1, -1),
    )


def solution(mesh):
    in_specs = (
        P(("groups", "bricks"), None, None, None),
        P(("groups", "bricks"), None),
        P(("groups", "bricks"), None),
        P(),
    )
    out_specs = P(("groups", "bricks"), None)
    return jax.shard_map(local, mesh=mesh, in_specs=in_specs, out_specs=out_specs, check_vma=False)
```
